256 devices in a mesh: dp: 2 (over core), row: 32 (over z, x), col: 4 (over y).
Axes of the slice: x: 4, y: 4, z: 8, core: 2. Of those that a mesh axis runs over, the one named last changes fastest.
Arguments:
- layer_input: bfloat16 [1024, 8192], P('dp', 'col'), may hold values from -6 to 6
- out_grad: bfloat16 [1024, 8192], P('dp', 'col'), may hold values from -6 to 6
- w_gate: bfloat16 [8192, 14336], P('col', 'row'), may hold values from -0.0625 to 0.0625
- w_up: bfloat16 [8192, 14336], P('col', 'row'), may hold values from -0.0625 to 0.0625
- w_down: bfloat16 [14336, 8192], P('row', 'col'), may hold values from -0.046875 to 0.046875
Outputs:
- in_grad: bfloat16 [1024, 8192], P('dp', 'col')
- gate_grad: bfloat16 [8192, 14336], P(('col', 'dp'), 'row')
- up_grad: bfloat16 [8192, 14336], P(('col', 'dp'), 'row')
- down_grad: bfloat16 [14336, 8192], P('row', ('col', 'dp'))
The draws below stay inside these ranges and needn't reach their ends.
All inputs are finite; a program needn't handle non-finite values.
Results may differ from the reference program's by a relative error of at most 0.0049.
Values may be sent and summed in bfloat16 or wider, within the bound.
A program may use at most 128 MiB of HBM per device.

```python
import jax
import jax.numpy as jnp

D = 8192
HID = 14336
TOKENS = 1024


def shard_levels(stream_key, extent, split, low, top_value):
    loudness, own = 1.0, jax.random.fold_in(stream_key, 6)
    for dim, parts in split:
        heights = jnp.exp(jax.random.uniform(jax.random.fold_in(own, dim), (parts,), jnp.float32, low / len(split), top_value / len(split)))
        loudness = loudness * jnp.repeat(heights, extent[dim] // parts).reshape([-1 if axis == dim else 1 for axis in range(len(extent))])
    return loudness


def centred(stream_key, dims, spread, reach, cuts=(), dtype=jnp.bfloat16):
    entries = jax.random.normal(stream_key, dims, jnp.float32) * spread
    if len(cuts) > 0:
        entries = shard_levels(stream_key, dims, cuts, -0.22, 0.18) * entries
    return jnp.clip(entries, min=-reach, max=reach).astype(dtype)


def setup_inputs(seed: int = 0) -> dict:
    keys = jax.random.split(jax.random.key(seed), 6)
    layer_input = centred(keys[0], (TOKENS, D), 1.0, 6.0, ((0, 2), (1, 4)))
    out_grad = centred(keys[1], (TOKENS, D), 1.0, 6.0, ((0, 2), (1, 4)))
    w_gate = centred(keys[2], (D, HID), D ** -0.5, 0.0625, ((0, 4), (1, 32)))
    w_up = centred(keys[3], (D, HID), D ** -0.5, 0.0625, ((0, 4), (1, 32)))
    w_down = centred(keys[4], (HID, D), HID ** -0.5, 0.046875, ((0, 32), (1, 4)))
    return {"layer_input": layer_input, "out_grad": out_grad, "w_gate": w_gate, "w_up": w_up, "w_down": w_down}


def swiglu_back(gate_pre, up_pre, hid_grad):
    sigmoid = jax.nn.sigmoid(gate_pre)
    activation = gate_pre * sigmoid
    hidden = (activation * up_pre).astype(jnp.bfloat16)
    up_delta = (hid_grad * activation).astype(jnp.bfloat16)
    gate_delta = (hid_grad * up_pre * sigmoid * (1.0 + gate_pre * (1.0 - sigmoid))).astype(jnp.bfloat16)
    return hidden, gate_delta, up_delta


def reference(layer_input, out_grad, w_gate, w_up, w_down):
    gate_pre = jnp.dot(layer_input, w_gate, preferred_element_type=jnp.float32)
    up_pre = jnp.dot(layer_input, w_up, preferred_element_type=jnp.float32)
    hid_grad = jnp.dot(out_grad, w_down.T, preferred_element_type=jnp.float32)
    hidden, gate_delta, up_delta = swiglu_back(gate_pre, up_pre, hid_grad)
    in_grad = (jnp.dot(gate_delta, w_gate.T, preferred_element_type=jnp.float32)
               + jnp.dot(up_delta, w_up.T, preferred_element_type=jnp.float32)).astype(jnp.bfloat16)
    gate_grad = jnp.dot(layer_input.T, gate_delta, preferred_element_type=jnp.float32).astype(jnp.bfloat16)
    up_grad = jnp.dot(layer_input.T, up_delta, preferred_element_type=jnp.float32).astype(jnp.bfloat16)
    down_grad = jnp.dot(hidden.T, out_grad, preferred_element_type=jnp.float32).astype(jnp.bfloat16)
    return in_grad, gate_grad, up_grad, down_grad
```

```python
import functools

import jax
import jax.numpy as jnp
from jax import lax
from jax.experimental import pallas as pl
from jax.experimental.pallas import tpu as pltpu
from jax.sharding import PartitionSpec as P

MESH = pl.DeviceIdType.MESH
BF16, F32 = jnp.bfloat16, jnp.float32
NX, NY, NZ = 4, 4, 8
TOK, WID, HID = 512, 2048, 448
CUT = 384
PACK = 3 * CUT + 256
HALF = WID // 2
ROUNDS = 2
SLAB = TOK // NY // ROUNDS
RTOK = TOK // ROUNDS
XCOL = WID // NX
ZROW = RTOK // NZ
ORDER = (
    ("f", 0), ("f", 1), ("s", 0), ("e", 0), ("e", 1), ("c", 0), ("c", 1), ("w", 0),
    ("x", 0), ("x", 1), ("w", 1), ("z", 0), ("z", 1), ("w", 2), ("a", 0), ("a", 1),
    ("o", 0), ("o", 1),
)


def dot(left, right, dims):
    return lax.dot_general(left, right, (dims, ((), ())), preferred_element_type=F32)


def pack(ref, first, second, third):
    dtype = ref.dtype
    for place, value in enumerate((first, second, third)):
        ref[:, place * CUT : (place + 1) * CUT] = value[:, :CUT].astype(dtype)
    tail = jnp.concatenate((first[:, CUT:], second[:, CUT:]), axis=1)
    ref[:, 3 * CUT : 3 * CUT + 128] = tail.astype(dtype)
    rest = jnp.concatenate((third[:, CUT:], jnp.zeros_like(third[:, CUT:])), axis=1)
    ref[:, 3 * CUT + 128 : PACK] = rest.astype(dtype)


def unpack(value):
    one, two = value[:, 3 * CUT : 3 * CUT + 128], value[:, 3 * CUT + 128 :]
    return (
        jnp.concatenate((value[:, :CUT], one[:, :64]), axis=1),
        jnp.concatenate((value[:, CUT : 2 * CUT], one[:, 64:]), axis=1),
        jnp.concatenate((value[:, 2 * CUT : 3 * CUT], two[:, :64]), axis=1),
    )


def kernel(
    x_hbm, g_hbm, wg_hbm, wu_hbm, wd_hbm, in_hbm, gate_hbm, up_hbm, down_hbm,
    xv, gv, wg, wu, wd, xs, gs, acc, ysend, yrecv, ag, agsib, delta, deltasib,
    xown, xsend, xrecv, zsend, zrecv, fin, gate_v, up_v, down_v,
    load_sem, out_sem, send_sem, recv_sem,
):
    dp, row, y = lax.axis_index("dp"), lax.axis_index("row"), lax.axis_index("col")
    z, x = row // NX, row % NX

    def at_y(k):
        return (dp, row, (y + k) % NY)

    def at_x(k):
        return (dp, z * NX + (x + k) % NX, y)

    def at_z(k):
        return (dp, ((z + k) % NZ) * NX + x, y)

    sibling = (1 - dp, row, y)

    barrier = pltpu.get_barrier_semaphore()
    partners = (
        [at_y(k) for k in range(1, NY)] + [at_x(k) for k in range(1, NX)] + [at_z(k) for k in range(1, NZ)] + [sibling]
    )
    for partner in partners:
        pl.semaphore_signal(barrier, inc=1, device_id=partner, device_id_type=MESH)

    loads = {}

    def load(name, src, dst):
        loads[name] = pltpu.make_async_copy(src, dst, load_sem.at[len(loads)])
        loads[name].start()

    def slab(p, k):
        return pl.ds(pl.multiple_of(((y + k) % NY) * (TOK // NY) + p * SLAB, SLAB), SLAB)

    def load_rows(name, src, dst, p):
        for k in range(NY):
            load((name, p, k), src.at[slab(p, k)], dst.at[pl.ds(p * RTOK + k * SLAB, SLAB)])

    load_rows("x", x_hbm, xv, 0)
    load("wg", wg_hbm, wg)
    load("wu", wu_hbm, wu)
    load_rows("g", g_hbm, gv, 0)
    load("wd", wd_hbm, wd)
    for p in range(1, ROUNDS):
        load_rows("x", x_hbm, xv, p)
        load_rows("g", g_hbm, gv, p)
    waited = set()

    def need(*names):
        for name in names:
            if name not in waited:
                waited.add(name)
                loads[name].wait()

    sends = {}

    def send(name, src, dst, device):
        n = len(sends)
        sends[name] = pltpu.make_async_remote_copy(
            src_ref=src, dst_ref=dst, send_sem=send_sem.at[n], recv_sem=recv_sem.at[n],
            device_id=device, device_id_type=MESH,
        )
        sends[name].start()

    def arrive(name):
        sends[name].wait_recv()

    outs = []

    def store(src, dst):
        outs.append(pltpu.make_async_copy(src, dst, out_sem.at[len(outs)]))
        outs[-1].start()

    def rows(p):
        return slice(p * RTOK, (p + 1) * RTOK)

    def forward(p):
        need(*[("x", p, k) for k in range(NY)], "wg")
        a = xv[rows(p)]
        gate = dot(a, wg[...], ((1,), (0,)))
        need("wu")
        up = dot(a, wu[...], ((1,), (0,)))
        need(*[("g", p, k) for k in range(NY)], "wd")
        hid = dot(gv[rows(p)], wd[...], ((1,), (1,)))
        pack(acc.at[p], gate[:SLAB], up[:SLAB], hid[:SLAB])
        pack(ysend.at[p], gate[SLAB:], up[SLAB:], hid[SLAB:])
        if p == 0:
            pl.semaphore_wait(barrier, len(partners))
        for k in (2, 1, 3):
            send(("yr", p, k), ysend.at[p, pl.ds((k - 1) * SLAB, SLAB)], yrecv.at[p, k - 1], at_y(k))

    def share(p):
        other = pl.ds(pl.multiple_of((1 - dp) * HALF, HALF), HALF)
        need(*[(name, q, k) for name in "xg" for q in range(ROUNDS) for k in range(NY)])
        send(("sx", 0), xv.at[:, other], xs, sibling)
        send(("sg", 0), gv.at[:, other], gs, sibling)

    def elementwise(p):
        for k in range(1, NY):
            arrive(("yr", p, k))
        gate, up, hid = unpack(
            acc[p] + yrecv[p, 0].astype(F32) + yrecv[p, 1].astype(F32) + yrecv[p, 2].astype(F32)
        )
        sig = jax.nn.sigmoid(gate)
        act = gate * sig
        pack(
            ag.at[p, pl.ds(0, SLAB)],
            hid * up * sig * (1.0 + gate * (1.0 - sig)), hid * act, act * up,
        )
        own = ag.at[p, pl.ds(0, SLAB)]
        for k in (2, 1, 3):
            send(("ya", p, k), own, ag.at[p, pl.ds((NY - k) * SLAB, SLAB)], at_y(k))

    def contract(p):
        for k in range(1, NY):
            arrive(("ya", p, k))
        send(("sd", p), ag.at[p], agsib.at[p], sibling)
        gd, ud, hd = unpack(ag[p])
        delta[0, rows(p)], delta[1, rows(p)], delta[2, rows(p)] = gd, ud, hd
        for k in (2, 1, 3, 0):
            block = pl.ds(pl.multiple_of(((x + k) % NX) * XCOL, XCOL), XCOL)
            part = dot(gd, wg[block, :], ((1,), (1,))) + dot(ud, wu[block, :], ((1,), (1,)))
            if k == 0:
                xown[p] = part
            else:
                xsend[p, k - 1] = part.astype(BF16)
                send(("xr", p, k), xsend.at[p, k - 1], xrecv.at[p, k - 1], at_x(k))

    def sum_x(p):
        for k in range(1, NX):
            arrive(("xr", p, k))
        xown[p] = xown[p] + xrecv[p, 0].astype(F32) + xrecv[p, 1].astype(F32) + xrecv[p, 2].astype(F32)
        for k in (4, 3, 5, 2, 6, 1, 7):
            part = pl.ds(pl.multiple_of(((z + k) % NZ) * ZROW, ZROW), ZROW)
            zsend[p, k - 1] = xown[p, part, :].astype(BF16)
            send(("zr", p, k), zsend.at[p, k - 1], zrecv.at[p, k - 1], at_z(k))

    def sum_z(p):
        for k in range(1, NZ):
            arrive(("zr", p, k))
        total = xown[p, pl.ds(pl.multiple_of(z * ZROW, ZROW), ZROW), :]
        for k in range(1, NZ):
            total = total + zrecv[p, k - 1].astype(F32)
        place = (
            pl.ds(pl.multiple_of(p * RTOK + z * ZROW, ZROW), ZROW),
            pl.ds(pl.multiple_of(x * XCOL, XCOL), XCOL),
        )
        fin[place] = total.astype(BF16)
        for k in (4, 3, 5, 2, 6, 1, 7):
            send(("za", p, k), fin.at[place], fin.at[place], at_z(k))

    def gather_x(p):
        for k in range(1, NZ):
            arrive(("za", p, k))
        place = fin.at[pl.ds(p * RTOK, RTOK), pl.ds(pl.multiple_of(x * XCOL, XCOL), XCOL)]
        for k in (2, 1, 3):
            send(("xa", p, k), place, place, at_x(k))

    def finish(p):
        for k in range(1, NX):
            arrive(("xa", p, k))
        for k in range(NY):
            store(fin.at[pl.ds(p * RTOK + k * SLAB, SLAB)], in_hbm.at[slab(p, k)])

    def weights(i):
        if i == 0:
            arrive(("sx", 0))
            arrive(("sg", 0))
            for p in range(ROUNDS):
                arrive(("sd", p))
                deltasib[0, rows(p)], deltasib[1, rows(p)], deltasib[2, rows(p)] = unpack(agsib[p])
        half = pl.ds(pl.multiple_of(dp * HALF, HALF), HALF)
        if i < 2:
            out, hbm = ((gate_v, gate_hbm), (up_v, up_hbm))[i]
            total = dot(xv[:, half], delta[i], ((0,), (0,))) + dot(xs[...], deltasib[i], ((0,), (0,)))
        else:
            out, hbm = down_v, down_hbm
            total = dot(delta[i], gv[:, half], ((0,), (0,))) + dot(deltasib[i], gs[...], ((0,), (0,)))
        out[...] = total.astype(BF16)
        store(out, hbm)

    tasks = {
        "f": forward, "s": share, "e": elementwise, "c": contract, "x": sum_x, "z": sum_z,
        "a": gather_x, "o": finish, "w": weights,
    }
    for name, i in ORDER:
        tasks[name](i)
    for copy in sends.values():
        copy.wait_send()
    for copy in outs:
        copy.wait()


def body(layer_input, out_grad, w_gate, w_up, w_down):
    n_sends = ROUNDS * (2 * (NY - 1) + 2 * (NX - 1) + 2 * (NZ - 1) + 1) + 2
    anywhere = pl.BlockSpec(memory_space=pl.ANY)
    return pl.pallas_call(
        kernel,
        out_shape=(
            jax.ShapeDtypeStruct((TOK, WID), BF16),
            jax.ShapeDtypeStruct((HALF, HID), BF16),
            jax.ShapeDtypeStruct((HALF, HID), BF16),
            jax.ShapeDtypeStruct((HID, HALF), BF16),
        ),
        in_specs=[anywhere] * 5,
        out_specs=[anywhere] * 4,
        scratch_shapes=[
            pltpu.VMEM((TOK, WID), BF16),
            pltpu.VMEM((TOK, WID), BF16),
            pltpu.VMEM((WID, HID), BF16),
            pltpu.VMEM((WID, HID), BF16),
            pltpu.VMEM((HID, WID), BF16),
            pltpu.VMEM((TOK, HALF), BF16),
            pltpu.VMEM((TOK, HALF), BF16),
            pltpu.VMEM((ROUNDS, SLAB, PACK), F32),
            pltpu.VMEM((ROUNDS, (NY - 1) * SLAB, PACK), BF16),
            pltpu.VMEM((ROUNDS, NY - 1, SLAB, PACK), BF16),
            pltpu.VMEM((ROUNDS, RTOK, PACK), BF16),
            pltpu.VMEM((ROUNDS, RTOK, PACK), BF16),
            pltpu.VMEM((3, TOK, HID), BF16),
            pltpu.VMEM((3, TOK, HID), BF16),
            pltpu.VMEM((ROUNDS, RTOK, XCOL), F32),
            pltpu.VMEM((ROUNDS, NX - 1, RTOK, XCOL), BF16),
            pltpu.VMEM((ROUNDS, NX - 1, RTOK, XCOL), BF16),
            pltpu.VMEM((ROUNDS, NZ - 1, ZROW, XCOL), BF16),
            pltpu.VMEM((ROUNDS, NZ - 1, ZROW, XCOL), BF16),
            pltpu.VMEM((TOK, WID), BF16),
            pltpu.VMEM((HALF, HID), BF16),
            pltpu.VMEM((HALF, HID), BF16),
            pltpu.VMEM((HID, HALF), BF16),
            pltpu.SemaphoreType.DMA((3 + 2 * NY * ROUNDS,)),
            pltpu.SemaphoreType.DMA((3 + NY * ROUNDS,)),
            pltpu.SemaphoreType.DMA((n_sends,)),
            pltpu.SemaphoreType.DMA((n_sends,)),
        ],
        compiler_params=pltpu.CompilerParams(
            collective_id=0, has_side_effects=True, vmem_limit_bytes=56 * 2**20
        ),
    )(layer_input, out_grad, w_gate, w_up, w_down)


def solution(mesh):
    placed = (P("dp", "col"), P("dp", "col"), P("col", "row"), P("col", "row"), P("row", "col"))
    return jax.shard_map(
        body,
        mesh=mesh,
        in_specs=placed,
        out_specs=(
            P("dp", "col"),
            P(("col", "dp"), "row"),
            P(("col", "dp"), "row"),
            P("row", ("col", "dp")),
        ),
        check_vma=False,
    )
```

```python
import functools

import jax
import jax.numpy as jnp
from jax import lax
from jax.experimental import pallas as pl
from jax.experimental.pallas import tpu as pltpu
from jax.sharding import PartitionSpec as P

MESH = pl.DeviceIdType.MESH
BF16, F32 = jnp.bfloat16, jnp.float32
NX, NY, NZ = 4, 4, 8
TOK, WID, HID = 512, 2048, 448
CUT = 384
PACK = 3 * CUT + 256
HALF = WID // 2
ROUNDS = 4
SLAB = TOK // NY // ROUNDS
RTOK = TOK // ROUNDS
XCOL = WID // NX
ZROW = RTOK // NZ
ORDER = (
    ("F", 0), ("F", 1), ("H", 0), ("Y", 0, 0), ("Y", 0, 1), ("Y", 1, 0), ("Y", 1, 1), ("E", 0), ("F", 2),
    ("E", 1), ("F", 3), ("G", 0, 0), ("G", 0, 1), ("Y", 2, 0), ("Y", 2, 1), ("G", 1, 0), ("G", 1, 1),
    ("Y", 3, 0), ("Y", 3, 1), ("C", 0), ("E", 2), ("C", 1), ("E", 3), ("X", 0, 0), ("X", 0, 1), ("G", 2, 0),
    ("G", 2, 1), ("X", 1, 0), ("X", 1, 1), ("G", 3, 0), ("G", 3, 1), ("C", 2), ("S", 0), ("C", 3), ("S", 1),
    ("W", 0), ("X", 2, 0), ("X", 2, 1), ("W", 1), ("W", 2), ("X", 3, 0), ("X", 3, 1), ("W", 3), ("T", 0),
    ("W", 4), ("W", 5), ("S", 2), ("T", 1), ("S", 3), ("A", 0), ("T", 2), ("B", 0, 0), ("B", 0, 1), ("A", 1),
    ("T", 3), ("O", 0), ("A", 2), ("B", 1, 0), ("B", 1, 1), ("A", 3), ("B", 2, 0), ("B", 2, 1), ("O", 1),
    ("B", 3, 0), ("B", 3, 1), ("O", 2), ("O", 3),
)


def dot(left, right, dims):
    return lax.dot_general(left, right, (dims, ((), ())), preferred_element_type=F32)


def pack(ref, first, second, third):
    dtype = ref.dtype
    for place, value in enumerate((first, second, third)):
        ref[:, place * CUT : (place + 1) * CUT] = value[:, :CUT].astype(dtype)
    tail = jnp.concatenate((first[:, CUT:], second[:, CUT:]), axis=1)
    ref[:, 3 * CUT : 3 * CUT + 128] = tail.astype(dtype)
    rest = jnp.concatenate((third[:, CUT:], jnp.zeros_like(third[:, CUT:])), axis=1)
    ref[:, 3 * CUT + 128 : PACK] = rest.astype(dtype)


def unpack(value):
    one, two = value[:, 3 * CUT : 3 * CUT + 128], value[:, 3 * CUT + 128 :]
    return (
        jnp.concatenate((value[:, :CUT], one[:, :64]), axis=1),
        jnp.concatenate((value[:, CUT : 2 * CUT], one[:, 64:]), axis=1),
        jnp.concatenate((value[:, 2 * CUT : 3 * CUT], two[:, :64]), axis=1),
    )


def kernel(
    x_hbm, g_hbm, wg_hbm, wu_hbm, wd_hbm, in_hbm, gate_hbm, up_hbm, down_hbm,
    xv, gv, wg, wu, wd, xs, gs, yown, yacc, ysend, yone, ytwo, ag, agsib, delta, deltasib,
    xown, xacc, xsend, xone, xtwo, zsend, zrecv, fin, gate_v, up_v, down_v,
    load_sem, out_sem, send_sem, recv_sem,
):
    dp, row, y = lax.axis_index("dp"), lax.axis_index("row"), lax.axis_index("col")
    z, x = row // NX, row % NX

    def at_y(k):
        return (dp, row, (y + k) % NY)

    def at_x(k):
        return (dp, z * NX + (x + k) % NX, y)

    def at_z(k):
        return (dp, ((z + k) % NZ) * NX + x, y)

    sibling = (1 - dp, row, y)

    barrier = pltpu.get_barrier_semaphore()
    partners = (
        [at_y(1), at_y(3), at_x(1), at_x(3)] + [at_z(k) for k in range(1, NZ)] + [sibling]
    )
    for partner in partners:
        pl.semaphore_signal(barrier, inc=1, device_id=partner, device_id_type=MESH)

    loads = {}

    def load(name, src, dst):
        loads[name] = pltpu.make_async_copy(src, dst, load_sem.at[len(loads)])
        loads[name].start()

    def slab(p, k):
        return pl.ds(pl.multiple_of(((y + k) % NY) * (TOK // NY) + p * SLAB, SLAB), SLAB)

    def load_rows(name, src, dst, p):
        for k in range(NY):
            load((name, p, k), src.at[slab(p, k)], dst.at[pl.ds(p * RTOK + k * SLAB, SLAB)])

    load_rows("x", x_hbm, xv, 0)
    load("wg", wg_hbm, wg)
    load("wu", wu_hbm, wu)
    load_rows("g", g_hbm, gv, 0)
    load("wd", wd_hbm, wd)
    for p in range(1, ROUNDS):
        load_rows("x", x_hbm, xv, p)
        load_rows("g", g_hbm, gv, p)
    waited = set()

    def need(*names):
        for name in names:
            if name not in waited:
                waited.add(name)
                loads[name].wait()

    sends = {}

    def send(name, src, dst, device):
        n = len(sends)
        sends[name] = pltpu.make_async_remote_copy(
            src_ref=src, dst_ref=dst, send_sem=send_sem.at[n], recv_sem=recv_sem.at[n],
            device_id=device, device_id_type=MESH,
        )
        sends[name].start()

    def arrive(name):
        sends[name].wait_recv()

    outs = []

    def store(src, dst):
        outs.append(pltpu.make_async_copy(src, dst, out_sem.at[len(outs)]))
        outs[-1].start()

    def rows(p):
        return slice(p * RTOK, (p + 1) * RTOK)

    def ring_start(tag, p, at, parts, one, two):
        h = parts[1].shape[0] // 2
        lo, hi = pl.ds(0, h), pl.ds(h, h)
        send((tag + "1", p, 0), parts[2].at[lo], one.at[p, 0], at(1))
        send((tag + "1", p, 1), parts[2].at[hi], one.at[p, 1], at(3))
        send((tag + "2", p, 0), parts[1].at[hi], two.at[p, 0, hi], at(1))
        send((tag + "2", p, 1), parts[3].at[lo], two.at[p, 1, lo], at(3))

    def ring_add(tag, p, way, at, part, acc, one, two):
        arrive((tag + "1", p, way))
        h = part.shape[0] // 2
        mine = pl.ds(way * h, h)
        part[mine, :] = (acc[p, way] + one[p, way].astype(F32)).astype(BF16)
        send((tag + "3", p, way), part.at[mine], two.at[p, way, mine], at(1 + 2 * way))

    def ring_sum(tag, p, own, two):
        for way in range(2):
            arrive((tag + "2", p, way))
            arrive((tag + "3", p, way))
        return own + two[p, 0].astype(F32) + two[p, 1].astype(F32)

    def yparts(p):
        return {k: ysend.at[p, k - 1] for k in (1, 2, 3)}

    def xparts(p):
        return {k: xsend.at[p, k - 1] for k in (1, 2, 3)}

    def forward(p):
        need(*[("x", p, k) for k in range(NY)], "wg")
        a = xv[rows(p)]
        gate = dot(a, wg[...], ((1,), (1,)))
        need("wu")
        up = dot(a, wu[...], ((1,), (1,)))
        need(*[("g", p, k) for k in range(NY)], "wd")
        hid = dot(gv[rows(p)], wd[...], ((1,), (1,)))

        def put(ref, start, stop):
            pack(ref, gate[start:stop], up[start:stop], hid[start:stop])

        for k in (2, 1, 3):
            put(ysend.at[p, k - 1], k * SLAB, (k + 1) * SLAB)
        if p == 0:
            pl.semaphore_wait(barrier, len(partners))
        ring_start("y", p, at_y, yparts(p), yone, ytwo)
        put(yacc.at[p, 0], SLAB, SLAB + SLAB // 2)
        put(yacc.at[p, 1], 3 * SLAB + SLAB // 2, 4 * SLAB)
        put(yown.at[p], 0, SLAB)

    def add_y(p, way):
        ring_add("y", p, way, at_y, yparts(p)[1 + 2 * way], yacc, yone, ytwo)

    def share(p):
        other = pl.ds(pl.multiple_of((1 - dp) * HALF, HALF), HALF)
        need(*[(name, q, k) for name in "xg" for q in range(ROUNDS) for k in range(NY)])
        send(("sx", 0), xv.at[:, other], xs, sibling)
        send(("sg", 0), gv.at[:, other], gs, sibling)

    def elementwise(p):
        gate, up, hid = unpack(ring_sum("y", p, yown[p], ytwo))
        sig = jax.nn.sigmoid(gate)
        act = gate * sig
        pack(
            ag.at[p, pl.ds(0, SLAB)],
            hid * up * sig * (1.0 + gate * (1.0 - sig)), hid * act, act * up,
        )
        own = ag.at[p, pl.ds(0, SLAB)]
        send(("g1", p, 0), own, ag.at[p, pl.ds(3 * SLAB, SLAB)], at_y(1))
        send(("g1", p, 1), own, ag.at[p, pl.ds(SLAB, SLAB)], at_y(3))

    def pass_y(p, way):
        arrive(("g1", p, way))
        h = SLAB // 2
        src = ag.at[p, pl.ds((3 - 2 * way) * SLAB + way * h, h)]
        send(("g2", p, way), src, ag.at[p, pl.ds(2 * SLAB + way * h, h)], at_y(1 + 2 * way))

    def contract(p):
        for way in range(2):
            arrive(("g2", p, way))
        send(("sd", p), ag.at[p], agsib.at[p], sibling)
        gd, ud, hd = unpack(ag[p])
        delta[0, rows(p)], delta[1, rows(p)], delta[2, rows(p)] = gd, ud, hd
        h = RTOK // 2
        for k in (2, 1, 3, 0):
            block = pl.ds(pl.multiple_of(((x + k) % NX) * XCOL, XCOL), XCOL)
            part = dot(gd, wg[:, block], ((1,), (0,))) + dot(ud, wu[:, block], ((1,), (0,)))
            if k == 0:
                xown[p] = part
            else:
                xsend[p, k - 1] = part.astype(BF16)
            if k == 1:
                xacc[p, 0] = part[:h]
            if k == 3:
                xacc[p, 1] = part[h:]
                ring_start("x", p, at_x, xparts(p), xone, xtwo)

    def add_x(p, way):
        ring_add("x", p, way, at_x, xparts(p)[1 + 2 * way], xacc, xone, xtwo)

    def sum_x(p):
        xown[p] = ring_sum("x", p, xown[p], xtwo)
        for k in (4, 3, 5, 2, 6, 1, 7):
            part = pl.ds(pl.multiple_of(((z + k) % NZ) * ZROW, ZROW), ZROW)
            zsend[p, k - 1] = xown[p, part, :].astype(BF16)
            send(("zr", p, k), zsend.at[p, k - 1], zrecv.at[p, k - 1], at_z(k))

    def sum_z(p):
        for k in range(1, NZ):
            arrive(("zr", p, k))
        total = xown[p, pl.ds(pl.multiple_of(z * ZROW, ZROW), ZROW), :]
        for k in range(1, NZ):
            total = total + zrecv[p, k - 1].astype(F32)
        place = (
            pl.ds(pl.multiple_of(p * RTOK + z * ZROW, ZROW), ZROW),
            pl.ds(pl.multiple_of(x * XCOL, XCOL), XCOL),
        )
        fin[place] = total.astype(BF16)
        for k in (4, 3, 5, 2, 6, 1, 7):
            send(("za", p, k), fin.at[place], fin.at[place], at_z(k))

    def xplace(p, k, start, size):
        return fin.at[
            pl.ds(p * RTOK + start, size),
            pl.ds(pl.multiple_of(((x + k) % NX) * XCOL, XCOL), XCOL),
        ]

    def gather_x(p):
        for k in range(1, NZ):
            arrive(("za", p, k))
        place = xplace(p, 0, 0, RTOK)
        for way in range(2):
            send(("b1", p, way), place, place, at_x(1 + 2 * way))

    def pass_x(p, way):
        arrive(("b1", p, way))
        h = RTOK // 2
        place = xplace(p, 3 - 2 * way, way * h, h)
        send(("b2", p, way), place, place, at_x(1 + 2 * way))

    def finish(p):
        for way in range(2):
            arrive(("b2", p, way))
        for k in range(NY):
            store(fin.at[pl.ds(p * RTOK + k * SLAB, SLAB)], in_hbm.at[slab(p, k)])

    def weights(i):
        if i == 0:
            arrive(("sx", 0))
            arrive(("sg", 0))
            for p in range(ROUNDS):
                arrive(("sd", p))
                deltasib[0, rows(p)], deltasib[1, rows(p)], deltasib[2, rows(p)] = unpack(agsib[p])
        i, j = i // 2, i % 2
        out, hbm = ((gate_v, gate_hbm), (up_v, up_hbm), (down_v, down_hbm))[i]
        own, sib = (gv, gs) if i == 2 else (xv, xs)
        w = HALF // 2
        half = pl.ds(pl.multiple_of(dp * HALF + j * w, w), w)
        part = pl.ds(j * w, w)
        total = dot(delta[i], own[:, half], ((0,), (0,))) + dot(deltasib[i], sib[:, part], ((0,), (0,)))
        out[:, part] = total.astype(BF16)
        if j == 1:
            store(out, hbm)

    tasks = {
        "F": forward, "H": share, "Y": add_y, "E": elementwise, "G": pass_y, "C": contract,
        "X": add_x, "S": sum_x, "T": sum_z, "A": gather_x, "B": pass_x, "O": finish, "W": weights,
    }
    for name, *args in ORDER:
        tasks[name](*args)
    for copy in sends.values():
        copy.wait_send()
    for copy in outs:
        copy.wait()


def body(layer_input, out_grad, w_gate, w_up, w_down):
    n_sends = ROUNDS * (2 * (6 + 4) + 2 * (NZ - 1) + 1) + 2
    anywhere = pl.BlockSpec(memory_space=pl.ANY)
    in_grad, gate_grad, up_grad, down_grad = pl.pallas_call(
        kernel,
        out_shape=(
            jax.ShapeDtypeStruct((TOK, WID), BF16),
            jax.ShapeDtypeStruct((HID, HALF), BF16),
            jax.ShapeDtypeStruct((HID, HALF), BF16),
            jax.ShapeDtypeStruct((HID, HALF), BF16),
        ),
        in_specs=[anywhere] * 5,
        out_specs=[anywhere] * 4,
        scratch_shapes=[
            pltpu.VMEM((TOK, WID), BF16),
            pltpu.VMEM((TOK, WID), BF16),
            pltpu.VMEM((HID, WID), BF16),
            pltpu.VMEM((HID, WID), BF16),
            pltpu.VMEM((HID, WID), BF16),
            pltpu.VMEM((TOK, HALF), BF16),
            pltpu.VMEM((TOK, HALF), BF16),
            pltpu.VMEM((ROUNDS, SLAB, PACK), F32),
            pltpu.VMEM((ROUNDS, 2, SLAB // 2, PACK), F32),
            pltpu.VMEM((ROUNDS, NY - 1, SLAB, PACK), BF16),
            pltpu.VMEM((ROUNDS, 2, SLAB // 2, PACK), BF16),
            pltpu.VMEM((ROUNDS, 2, SLAB, PACK), BF16),
            pltpu.VMEM((ROUNDS, RTOK, PACK), BF16),
            pltpu.VMEM((ROUNDS, RTOK, PACK), BF16),
            pltpu.VMEM((3, TOK, HID), BF16),
            pltpu.VMEM((3, TOK, HID), BF16),
            pltpu.VMEM((ROUNDS, RTOK, XCOL), F32),
            pltpu.VMEM((ROUNDS, 2, RTOK // 2, XCOL), F32),
            pltpu.VMEM((ROUNDS, NX - 1, RTOK, XCOL), BF16),
            pltpu.VMEM((ROUNDS, 2, RTOK // 2, XCOL), BF16),
            pltpu.VMEM((ROUNDS, 2, RTOK, XCOL), BF16),
            pltpu.VMEM((ROUNDS, NZ - 1, ZROW, XCOL), BF16),
            pltpu.VMEM((ROUNDS, NZ - 1, ZROW, XCOL), BF16),
            pltpu.VMEM((TOK, WID), BF16),
            pltpu.VMEM((HID, HALF), BF16),
            pltpu.VMEM((HID, HALF), BF16),
            pltpu.VMEM((HID, HALF), BF16),
            pltpu.SemaphoreType.DMA((3 + 2 * NY * ROUNDS,)),
            pltpu.SemaphoreType.DMA((3 + NY * ROUNDS,)),
            pltpu.SemaphoreType.DMA((n_sends,)),
            pltpu.SemaphoreType.DMA((n_sends,)),
        ],
        compiler_params=pltpu.CompilerParams(
            collective_id=0, has_side_effects=True, vmem_limit_bytes=56 * 2**20
        ),
    )(layer_input, out_grad, w_gate.T, w_up.T, w_down)
    return in_grad, gate_grad.T, up_grad.T, down_grad


def solution(mesh):
    placed = (P("dp", "col"), P("dp", "col"), P("col", "row"), P("col", "row"), P("row", "col"))
    return jax.shard_map(
        body,
        mesh=mesh,
        in_specs=placed,
        out_specs=(
            P("dp", "col"),
            P(("col", "dp"), "row"),
            P(("col", "dp"), "row"),
            P("row", ("col", "dp")),
        ),
        check_vma=False,
    )
```

```python
import jax
import jax.numpy as jnp
from jax import lax
from jax.experimental import pallas as pl
from jax.experimental.pallas import tpu as pltpu
from jax.sharding import PartitionSpec as P

MESH = pl.DeviceIdType.MESH
BF16, F32 = jnp.bfloat16, jnp.float32
NX, NY, NZ = 4, 4, 8
TOK, WID, HID = 512, 2048, 448
CUT = 384
BOTH = 2 * HID
PACK = BOTH + 512
HALF = WID // 2
OWN = TOK // NY
ROUNDS = 8
BATCHES = ((0,), (1, 2), (3, 4), (5, 6, 7))
SLAB = OWN // ROUNDS
RTOK = TOK // ROUNDS
XCOL = WID // NX
ZROW, ZCOL = RTOK // 2, XCOL // 4
EARLY = len(BATCHES[0]) * SLAB
PAIR = 2
XSUM = (1, 0, 0, 0, 0, 0, 1, 0)
XGATHER = (1, 1, 0, 0, 1, 0, 0, 1)
ORDER = (
    ("F", 0), ("F", 1), ("H",), ("E", 0), ("F", 2), ("E", 1), ("E", 2), ("C", 0), ("E", 3), ("F", 3), ("E", 4),
    ("X", 0, 0), ("X", 0, 1), ("C", 1), ("C", 2), ("C", 3), ("S", 0), ("E", 5), ("E", 6), ("S", 1), ("E", 7),
    ("S", 2), ("C", 4), ("T", 0), ("C", 5), ("C", 6), ("S", 3), ("T", 1), ("C", 7), ("K",), ("T", 2), ("S", 4),
    ("W", 0), ("A", 0), ("W", 1), ("S", 5), ("X", 6, 0), ("X", 6, 1), ("T", 3), ("W", 2), ("A", 1), ("A", 2),
    ("S", 7), ("L",), ("T", 4), ("B", 0, 0), ("B", 0, 1), ("S", 6), ("T", 5), ("W", 3), ("B", 1, 0),
    ("B", 1, 1), ("A", 3), ("O", 2), ("T", 7), ("O", 0), ("A", 4), ("O", 1), ("T", 6), ("A", 5), ("O", 3),
    ("B", 4, 0), ("B", 4, 1), ("A", 7), ("A", 6), ("O", 5), ("O", 4), ("B", 7, 0), ("B", 7, 1), ("O", 6),
    ("O", 7),
)


def dot(left, right, dims):
    return lax.dot_general(left, right, (dims, ((), ())), preferred_element_type=F32)


def kernel(
    x_hbm, g_hbm, wg_hbm, wu_hbm, wd_hbm, fin, gate_v, up_v, down_v,
    xv, gv, wgu, wd, xs, gs, yown, ysend, yrecv, ag, agsib, hall, hsib,
    xown, xacc, xsend, xone, xtwo, zsend, zrecv, load_sem, send_sem, recv_sem,
):
    dp, row, y = lax.axis_index("dp"), lax.axis_index("row"), lax.axis_index("col")
    z, x = row // NX, row % NX

    def at_y(k):
        return (dp, row, (y + k) % NY)

    def at_x(k):
        return (dp, z * NX + (x + k) % NX, y)

    def at_z(k):
        return (dp, ((z + k) % NZ) * NX + x, y)

    sibling = (1 - dp, row, y)

    barrier = pltpu.get_barrier_semaphore()
    partners = (
        [at_y(k) for k in range(1, NY)] + [at_x(k) for k in range(1, NX)] + [at_z(k) for k in range(1, NZ)] + [sibling]
    )
    for partner in partners:
        pl.semaphore_signal(barrier, inc=1, device_id=partner, device_id_type=MESH)

    loads = {}

    def load(name, src, dst):
        n = loads.setdefault(name, len(loads))
        pltpu.make_async_copy(src, dst, load_sem.at[n]).start()

    def loaded(name, ref):
        if name in loads:
            pltpu.make_async_copy(ref, ref, load_sem.at[loads.pop(name)]).wait()

    early, late = pl.ds(0, EARLY), pl.ds(EARLY, OWN - EARLY)
    rest = HID - CUT
    load("x0", x_hbm.at[:, early], xv.at[:, early])
    load("w", wg_hbm.at[pl.ds(0, CUT)], wgu.at[pl.ds(0, CUT)])
    load("w", wu_hbm.at[pl.ds(0, CUT)], wgu.at[pl.ds(CUT, CUT)])
    load("w", wg_hbm.at[pl.ds(CUT, rest)], wgu.at[pl.ds(2 * CUT, rest)])
    load("w", wu_hbm.at[pl.ds(CUT, rest)], wgu.at[pl.ds(CUT + HID, rest)])
    load("g0", g_hbm.at[:, early], gv.at[:, early])
    load("wd", wd_hbm, wd)
    load("x1", x_hbm.at[:, late], xv.at[:, late])
    load("g1", g_hbm.at[:, late], gv.at[:, late])

    sent, received = {}, {}

    def send(out, name, src, dst, device):
        n, m = sent.setdefault(out, len(sent)), received.setdefault(name, len(received))
        pltpu.make_async_remote_copy(
            src_ref=src, dst_ref=dst, send_sem=send_sem.at[n], recv_sem=recv_sem.at[m],
            device_id=device, device_id_type=MESH,
        ).start()

    def arrive(name, ref):
        pltpu.make_async_copy(ref, ref, recv_sem.at[received[name]]).wait()

    def slab(p):
        return pl.ds(p * SLAB, SLAB)

    def forward(i):
        first, n = BATCHES[i][0], len(BATCHES[i]) * SLAB
        part = pl.ds(first * SLAB, n)
        loaded("x0", xv.at[:, early])
        loaded("w", wgu)
        if i > 0:
            loaded("x1", xv.at[:, late])
        a = jnp.concatenate([xv[(y + k) % NY, part] for k in range(NY)], axis=0)
        both = dot(a, wgu[...], ((1,), (1,)))
        loaded("g0", gv.at[:, early])
        loaded("wd", wd)
        if i > 0:
            loaded("g1", gv.at[:, late])
        a = jnp.concatenate([gv[(y + k) % NY, part] for k in range(NY)], axis=0)
        hid = dot(a, wd[...], ((1,), (1,)))
        hid = jnp.concatenate((hid, jnp.zeros((NY * n, PACK - BOTH - HID), F32)), axis=1)
        for p in BATCHES[i]:
            start = (p - first) * SLAB
            for k in range(1, NY):
                mine = slice(k * n + start, k * n + start + SLAB)
                ysend[p, k - 1, :, :BOTH] = both[mine].astype(BF16)
                ysend[p, k - 1, :, BOTH:] = hid[mine].astype(BF16)
            if p == 0:
                pl.semaphore_wait(barrier, len(partners))
            for k in (2, 1, 3):
                send("yr", ("yr", p), ysend.at[p, k - 1], yrecv.at[p, k - 1], at_y(k))
            yown[p, :, :BOTH] = both[start : start + SLAB]
            yown[p, :, BOTH:] = hid[start : start + SLAB]

    def share():
        other = pl.ds(pl.multiple_of((1 - dp) * HALF, HALF), HALF)
        send("sx", "sx", xv.at[:, :, other], xs, sibling)
        send("sg", "sg", gv.at[:, :, other], gs, sibling)

    def swiglu_back(gate, up, hid):
        sig = jax.nn.sigmoid(gate)
        act = gate * sig
        return (
            (act * up).astype(BF16),
            (hid * up * sig * (1.0 + gate * (1.0 - sig))).astype(BF16),
            (hid * act).astype(BF16),
        )

    def elementwise(p):
        arrive(("yr", p), yrecv.at[p])
        total = yown[p] + yrecv[p, 0].astype(F32) + yrecv[p, 1].astype(F32) + yrecv[p, 2].astype(F32)
        hidden, gate, up = swiglu_back(
            total[:, :CUT], total[:, CUT : 2 * CUT], total[:, BOTH : BOTH + CUT]
        )
        ag[y, slab(p), :CUT] = gate
        ag[y, slab(p), CUT : 2 * CUT] = up
        hall[y, slab(p), :CUT] = hidden
        rest = HID - CUT
        hidden, gate, up = swiglu_back(
            total[:, 2 * CUT : 2 * CUT + rest], total[:, 2 * CUT + rest : BOTH], total[:, BOTH + CUT : BOTH + HID]
        )
        ag[y, slab(p), 2 * CUT :] = jnp.concatenate((gate, up), axis=1)
        hall[y, slab(p), CUT:] = jnp.concatenate((hidden, jnp.zeros_like(hidden)), axis=1)
        own = ag.at[y, slab(p)]
        for k in (2, 1, 3):
            send("yg", ("yg", p), own, own, at_y(k))

    def hidden_send():
        for k in (2, 1, 3):
            send("hg", "hg", hall.at[y], hall.at[y], at_y(k))

    def hidden_share():
        arrive("hg", hall.at[pl.ds(0, NY - 1)])
        send("hs", "hs", hall, hsib, sibling)

    def contract(p):
        arrive(("yg", p), ag.at[pl.ds(0, NY - 1), slab(p)])
        if p % PAIR == PAIR - 1:
            part = pl.ds((p - PAIR + 1) * SLAB, PAIR * SLAB)
            send("sd", "sd", ag.at[:, part], agsib.at[:, part], sibling)
        a = jnp.concatenate([ag[k, slab(p)] for k in range(NY)], axis=0)
        h = RTOK // 2
        lo, hi = pl.ds(0, h), pl.ds(h, h)
        for k in (2, 1, 3, 0):
            block = pl.ds(pl.multiple_of(((x + k) % NX) * XCOL, XCOL), XCOL)
            part = dot(a, wgu[:, block], ((1,), (0,)))
            if k == 0:
                xown[p] = part
                continue
            out = xsend.at[p, k - 1]
            out[...] = part.astype(BF16)
            if not XSUM[p]:
                send("xr", ("xr", p), out, xtwo.at[p, k - 1], at_x(k))
            elif k == 2:
                send("xr", ("x1", p, 0), out.at[lo], xone.at[p, 0], at_x(1))
                send("xr", ("x1", p, 1), out.at[hi], xone.at[p, 1], at_x(3))
            elif k == 1:
                xacc[p, 0] = part[:h]
                send("xr", ("xr", p), out.at[hi], xtwo.at[p, 0, hi], at_x(1))
            else:
                xacc[p, 1] = part[h:]
                send("xr", ("xr", p), out.at[lo], xtwo.at[p, 1, lo], at_x(3))

    def add_x(p, way):
        arrive(("x1", p, way), xone.at[p, way])
        h = RTOK // 2
        mine = pl.ds(way * h, h)
        out = xsend.at[p, 2 * way, mine]
        out[...] = (xacc[p, way] + xone[p, way].astype(F32)).astype(BF16)
        send("xr", ("xr", p), out, xtwo.at[p, way, mine], at_x(1 + 2 * way))

    def zplace(p, part):
        return (
            pl.ds(2 * (part // 4), 2),
            slab(p),
            pl.ds(pl.multiple_of(x * XCOL + (part % 4) * ZCOL, ZCOL), ZCOL),
        )

    def sum_x(p):
        if XSUM[p]:
            arrive(("xr", p), xtwo.at[p, pl.ds(0, 2)])
            total = xown[p] + xtwo[p, 0].astype(F32) + xtwo[p, 1].astype(F32)
        else:
            arrive(("xr", p), xtwo.at[p])
            total = xown[p] + xtwo[p, 0].astype(F32) + xtwo[p, 1].astype(F32) + xtwo[p, 2].astype(F32)
        xown[p] = total
        for k in (4, 3, 5, 2, 6, 1, 7):
            part = (z + k) % NZ
            zsend[p, k - 1] = xown[
                p,
                pl.ds(pl.multiple_of((part // 4) * ZROW, ZROW), ZROW),
                pl.ds(pl.multiple_of((part % 4) * ZCOL, ZCOL), ZCOL),
            ].astype(BF16)
            send("zr", ("zr", p), zsend.at[p, k - 1], zrecv.at[p, k - 1], at_z(k))

    def sum_z(p):
        arrive(("zr", p), zrecv.at[p])
        total = xown[
            p,
            pl.ds(pl.multiple_of((z // 4) * ZROW, ZROW), ZROW),
            pl.ds(pl.multiple_of((z % 4) * ZCOL, ZCOL), ZCOL),
        ]
        for k in range(1, NZ):
            total = total + zrecv[p, k - 1].astype(F32)
        place = zplace(p, z)
        fin[place] = total.astype(BF16).reshape(2, SLAB, ZCOL)
        for k in (4, 3, 5, 2, 6, 1, 7):
            send("za", ("za", p), fin.at[place], fin.at[place], at_z(k))

    def xplace(p, k, start, size):
        return fin.at[
            pl.ds(start, size), slab(p), pl.ds(pl.multiple_of(((x + k) % NX) * XCOL, XCOL), XCOL)
        ]

    def gather_x(p):
        arrive(("za", p), zrecv.at[p])
        place = xplace(p, 0, 0, NY)
        for k in (1, 3) if XGATHER[p] else (2, 1, 3):
            send("xg", ("xg", p, k) if XGATHER[p] else ("xg", p), place, place, at_x(k))

    def pass_x(p, way):
        arrive(("xg", p, 1 + 2 * way), xplace(p, 3 - 2 * way, 0, NY))
        place = xplace(p, 3 - 2 * way, 2 * way, 2)
        send("xg", ("xh", p), place, place, at_x(1 + 2 * way))

    def finish(p):
        if XGATHER[p]:
            arrive(("xh", p), xplace(p, 2, 0, NY))
        else:
            arrive(("xg", p), xtwo.at[p])

    def weights(i):
        if i == 0:
            arrive("sx", xs)
            arrive("sg", gs)
            arrive("sd", agsib)
        if i == 3:
            arrive("hs", hsib)
        half = pl.ds(pl.multiple_of(dp * HALF, HALF), HALF)
        start, size = ((0, CUT), (CUT, CUT), (2 * CUT, BOTH - 2 * CUT), (0, HID))[i]
        mine, theirs, own, sib = (hall, hsib, gv, gs) if i == 3 else (ag, agsib, xv, xs)
        cols = slice(start, start + size)
        total = dot(mine[:, :, cols].reshape(TOK, size), own[:, :, half].reshape(TOK, HALF), ((0,), (0,)))
        total += dot(theirs[:, :, cols].reshape(TOK, size), sib[...].reshape(TOK, HALF), ((0,), (0,)))
        total = total.astype(BF16)
        if i == 2:
            gate_v[CUT:, :] = total[:rest]
            up_v[CUT:, :] = total[rest:]
        else:
            (gate_v, up_v, None, down_v)[i][:size, :] = total

    tasks = {
        "F": forward, "H": share, "E": elementwise, "K": hidden_send, "L": hidden_share, "C": contract,
        "X": add_x, "S": sum_x, "T": sum_z, "A": gather_x, "B": pass_x, "O": finish, "W": weights,
    }
    for name, *args in ORDER:
        tasks[name](*args)
    for out, ref in (
        ("yr", ysend), ("yg", ag.at[pl.ds(0, NY - 1)]), ("hg", hall.at[pl.ds(0, NY - 1)]), ("xr", xsend),
        ("zr", zsend), ("za", zrecv), ("xg", xsend), ("sx", xs), ("sg", gs), ("sd", agsib), ("hs", hsib),
    ):
        pltpu.make_async_copy(ref, ref, send_sem.at[sent[out]]).wait()


def body(layer_input, out_grad, w_gate, w_up, w_down):
    n_received = 5 + 4 * ROUNDS + sum(3 if ring else 1 for ring in XSUM + XGATHER)
    in_grad, gate_grad, up_grad, down_grad = pl.pallas_call(
        kernel,
        out_shape=(
            pltpu.VMEM((NY, OWN, WID), BF16),
            pltpu.VMEM((HID, HALF), BF16),
            pltpu.VMEM((HID, HALF), BF16),
            pltpu.VMEM((HID, HALF), BF16),
        ),
        in_specs=[pl.BlockSpec(memory_space=pltpu.HBM)] * 5,
        out_specs=[pl.BlockSpec(memory_space=pltpu.VMEM)] * 4,
        scratch_shapes=[
            pltpu.VMEM((NY, OWN, WID), BF16),
            pltpu.VMEM((NY, OWN, WID), BF16),
            pltpu.VMEM((BOTH, WID), BF16),
            pltpu.VMEM((HID, WID), BF16),
            pltpu.VMEM((NY, OWN, HALF), BF16),
            pltpu.VMEM((NY, OWN, HALF), BF16),
            pltpu.VMEM((ROUNDS, SLAB, PACK), F32),
            pltpu.VMEM((ROUNDS, NY - 1, SLAB, PACK), BF16),
            pltpu.VMEM((ROUNDS, NY - 1, SLAB, PACK), BF16),
            pltpu.VMEM((NY, OWN, BOTH), BF16),
            pltpu.VMEM((NY, OWN, BOTH), BF16),
            pltpu.VMEM((NY, OWN, PACK - BOTH), BF16),
            pltpu.VMEM((NY, OWN, PACK - BOTH), BF16),
            pltpu.VMEM((ROUNDS, RTOK, XCOL), F32),
            pltpu.VMEM((ROUNDS, 2, RTOK // 2, XCOL), F32),
            pltpu.VMEM((ROUNDS, NX - 1, RTOK, XCOL), BF16),
            pltpu.VMEM((ROUNDS, 2, RTOK // 2, XCOL), BF16),
            pltpu.VMEM((ROUNDS, NX - 1, RTOK, XCOL), BF16),
            pltpu.VMEM((ROUNDS, NZ - 1, ZROW, ZCOL), BF16),
            pltpu.VMEM((ROUNDS, NZ - 1, ZROW, ZCOL), BF16),
            pltpu.SemaphoreType.DMA((6,)),
            pltpu.SemaphoreType.DMA((11,)),
            pltpu.SemaphoreType.DMA((n_received,)),
        ],
        compiler_params=pltpu.CompilerParams(
            collective_id=0, has_side_effects=True, vmem_limit_bytes=58 * 2**20
        ),
    )(
        layer_input.reshape(NY, OWN, WID), out_grad.reshape(NY, OWN, WID), w_gate.T, w_up.T, w_down,
    )
    return in_grad.reshape(TOK, WID), gate_grad.T, up_grad.T, down_grad


def solution(mesh):
    placed = (P("dp", "col"), P("dp", "col"), P("col", "row"), P("col", "row"), P("row", "col"))
    return jax.shard_map(
        body,
        mesh=mesh,
        in_specs=placed,
        out_specs=(
            P("dp", "col"),
            P(("col", "dp"), "row"),
            P(("col", "dp"), "row"),
            P("row", ("col", "dp")),
        ),
        check_vma=False,
    )
```

```python
import jax
import jax.numpy as jnp
from jax import lax
from jax.experimental import pallas as pl
from jax.experimental.pallas import tpu as pltpu
from jax.sharding import PartitionSpec as P

MESH = pl.DeviceIdType.MESH
BF16, F32 = jnp.bfloat16, jnp.float32
NX, NY, NZ = 4, 4, 8
TOK, WID, HID = 512, 2048, 448
CUT = 384
BOTH = 2 * HID
PACK = BOTH + 512
HALF = WID // 2
OWN = TOK // NY
ROUNDS = 8
BATCHES = ((0,), (1, 2), (3, 4), (5, 6), (7,))
SLAB = OWN // ROUNDS
RTOK = TOK // ROUNDS
XCOL = WID // NX
ZROW, ZCOL = RTOK // 2, XCOL // 4
EARLY = len(BATCHES[0]) * SLAB
PAIR = 2
XSUM = (1, 1, 0, 0, 0, 0, 0, 0)
XGATHER = (1, 1, 1, 0, 1, 1, 1, 0)
ORDER = (
    ("F", 0), ("F", 1), ("H",), ("E", 0), ("E", 1), ("F", 2), ("E", 2), ("C", 0), ("C", 1), ("E", 3), ("F", 3),
    ("X", 0, 0), ("X", 0, 1), ("E", 4), ("X", 1, 0), ("X", 1, 1), ("C", 2), ("C", 3), ("S", 0), ("S", 1),
    ("E", 5), ("F", 4), ("E", 6), ("S", 2), ("C", 4), ("C", 5), ("T", 0), ("S", 3), ("T", 1), ("E", 7),
    ("C", 6), ("T", 2), ("S", 4), ("C", 7), ("K",), ("A", 0), ("S", 5), ("T", 3), ("W", 0), ("W", 1), ("S", 6),
    ("W", 2), ("A", 1), ("A", 2), ("T", 4), ("S", 7), ("T", 5), ("B", 0, 0), ("B", 0, 1), ("A", 3), ("L",),
    ("B", 1, 0), ("B", 1, 1), ("T", 6), ("W", 3), ("O", 0), ("B", 2, 0), ("B", 2, 1), ("A", 4), ("T", 7),
    ("A", 5), ("O", 3), ("O", 1), ("A", 6), ("O", 2), ("B", 4, 0), ("B", 4, 1), ("A", 7), ("B", 5, 0),
    ("B", 5, 1), ("B", 6, 0), ("B", 6, 1), ("O", 4), ("O", 7), ("O", 5), ("O", 6),
)


def dot(left, right, dims):
    return lax.dot_general(left, right, (dims, ((), ())), preferred_element_type=F32)


def kernel(
    x_hbm, g_hbm, wg_hbm, wu_hbm, wd_hbm, fin, gate_v, up_v, down_v,
    xv, gv, wgu, wd, xs, gs, yown, ysend, yrecv, ag, agsib, hall, hsib,
    xown, xacc, xsend, xone, xtwo, zsend, zrecv, load_sem, send_sem, recv_sem,
):
    dp, row, y = lax.axis_index("dp"), lax.axis_index("row"), lax.axis_index("col")
    z, x = row // NX, row % NX

    def at_y(k):
        return (dp, row, (y + k) % NY)

    def at_x(k):
        return (dp, z * NX + (x + k) % NX, y)

    def at_z(k):
        return (dp, ((z + k) % NZ) * NX + x, y)

    sibling = (1 - dp, row, y)

    barrier = pltpu.get_barrier_semaphore()
    partners = (
        [at_y(k) for k in range(1, NY)] + [at_x(k) for k in range(1, NX)] + [at_z(k) for k in range(1, NZ)] + [sibling]
    )
    for partner in partners:
        pl.semaphore_signal(barrier, inc=1, device_id=partner, device_id_type=MESH)

    loads = {}

    def load(name, src, dst):
        n = loads.setdefault(name, len(loads))
        pltpu.make_async_copy(src, dst, load_sem.at[n]).start()

    def loaded(name, ref):
        if name in loads:
            pltpu.make_async_copy(ref, ref, load_sem.at[loads.pop(name)]).wait()

    early, late = pl.ds(0, EARLY), pl.ds(EARLY, OWN - EARLY)
    rest = HID - CUT
    load("x0", x_hbm.at[:, early], xv.at[:, early])
    load("w", wg_hbm.at[pl.ds(0, CUT)], wgu.at[pl.ds(0, CUT)])
    load("w", wu_hbm.at[pl.ds(0, CUT)], wgu.at[pl.ds(CUT, CUT)])
    load("w", wg_hbm.at[pl.ds(CUT, rest)], wgu.at[pl.ds(2 * CUT, rest)])
    load("w", wu_hbm.at[pl.ds(CUT, rest)], wgu.at[pl.ds(CUT + HID, rest)])
    load("g0", g_hbm.at[:, early], gv.at[:, early])
    load("wd", wd_hbm, wd)
    load("x1", x_hbm.at[:, late], xv.at[:, late])
    load("g1", g_hbm.at[:, late], gv.at[:, late])

    sent, received = {}, {}

    def send(out, name, src, dst, device):
        n, m = sent.setdefault(out, len(sent)), received.setdefault(name, len(received))
        pltpu.make_async_remote_copy(
            src_ref=src, dst_ref=dst, send_sem=send_sem.at[n], recv_sem=recv_sem.at[m],
            device_id=device, device_id_type=MESH,
        ).start()

    def arrive(name, ref):
        pltpu.make_async_copy(ref, ref, recv_sem.at[received[name]]).wait()

    def slab(p):
        return pl.ds(p * SLAB, SLAB)

    def forward(i):
        first, n = BATCHES[i][0], len(BATCHES[i]) * SLAB
        part = pl.ds(first * SLAB, n)
        loaded("x0", xv.at[:, early])
        loaded("w", wgu)
        if i > 0:
            loaded("x1", xv.at[:, late])
        a = jnp.concatenate([xv[(y + k) % NY, part] for k in range(NY)], axis=0)
        both = dot(a, wgu[...], ((1,), (1,)))
        loaded("g0", gv.at[:, early])
        loaded("wd", wd)
        if i > 0:
            loaded("g1", gv.at[:, late])
        a = jnp.concatenate([gv[(y + k) % NY, part] for k in range(NY)], axis=0)
        hid = dot(a, wd[...], ((1,), (1,)))
        hid = jnp.concatenate((hid, jnp.zeros((NY * n, PACK - BOTH - HID), F32)), axis=1)
        for p in BATCHES[i]:
            start = (p - first) * SLAB
            for k in range(1, NY):
                mine = slice(k * n + start, k * n + start + SLAB)
                ysend[p, k - 1, :, :BOTH] = both[mine].astype(BF16)
                ysend[p, k - 1, :, BOTH:] = hid[mine].astype(BF16)
            if p == 0:
                pl.semaphore_wait(barrier, len(partners))
            for k in (2, 1, 3):
                send("yr", ("yr", p), ysend.at[p, k - 1], yrecv.at[p, k - 1], at_y(k))
            yown[p, :, :BOTH] = both[start : start + SLAB]
            yown[p, :, BOTH:] = hid[start : start + SLAB]

    def share():
        other = pl.ds(pl.multiple_of((1 - dp) * HALF, HALF), HALF)
        send("sx", "sx", xv.at[:, :, other], xs, sibling)
        send("sg", "sg", gv.at[:, :, other], gs, sibling)

    def swiglu_back(gate, up, hid):
        sig = jax.nn.sigmoid(gate)
        act = gate * sig
        return (
            (act * up).astype(BF16),
            (hid * up * sig * (1.0 + gate * (1.0 - sig))).astype(BF16),
            (hid * act).astype(BF16),
        )

    def elementwise(p):
        arrive(("yr", p), yrecv.at[p])
        total = yown[p] + yrecv[p, 0].astype(F32) + yrecv[p, 1].astype(F32) + yrecv[p, 2].astype(F32)
        hidden, gate, up = swiglu_back(
            total[:, :CUT], total[:, CUT : 2 * CUT], total[:, BOTH : BOTH + CUT]
        )
        ag[y, slab(p), :CUT] = gate
        ag[y, slab(p), CUT : 2 * CUT] = up
        hall[y, slab(p), :CUT] = hidden
        rest = HID - CUT
        hidden, gate, up = swiglu_back(
            total[:, 2 * CUT : 2 * CUT + rest], total[:, 2 * CUT + rest : BOTH], total[:, BOTH + CUT : BOTH + HID]
        )
        ag[y, slab(p), 2 * CUT :] = jnp.concatenate((gate, up), axis=1)
        hall[y, slab(p), CUT:] = jnp.concatenate((hidden, jnp.zeros_like(hidden)), axis=1)
        own = ag.at[y, slab(p)]
        for k in (2, 1, 3):
            send("yg", ("yg", p), own, own, at_y(k))

    def hidden_send():
        for k in (2, 1, 3):
            send("hg", "hg", hall.at[y], hall.at[y], at_y(k))

    def hidden_share():
        arrive("hg", hall.at[pl.ds(0, NY - 1)])
        send("hs", "hs", hall, hsib, sibling)

    def contract(p):
        arrive(("yg", p), ag.at[pl.ds(0, NY - 1), slab(p)])
        if p % PAIR == PAIR - 1:
            part = pl.ds((p - PAIR + 1) * SLAB, PAIR * SLAB)
            send("sd", "sd", ag.at[:, part], agsib.at[:, part], sibling)
        a = jnp.concatenate([ag[k, slab(p)] for k in range(NY)], axis=0)
        h = RTOK // 2
        lo, hi = pl.ds(0, h), pl.ds(h, h)
        for k in (2, 1, 3, 0):
            block = pl.ds(pl.multiple_of(((x + k) % NX) * XCOL, XCOL), XCOL)
            part = dot(a, wgu[:, block], ((1,), (0,)))
            if k == 0:
                xown[p] = part
                continue
            out = xsend.at[p, k - 1]
            out[...] = part.astype(BF16)
            if not XSUM[p]:
                send("xr", ("xr", p), out, xtwo.at[p, k - 1], at_x(k))
            elif k == 2:
                send("xr", ("x1", p, 0), out.at[lo], xone.at[p, 0], at_x(1))
                send("xr", ("x1", p, 1), out.at[hi], xone.at[p, 1], at_x(3))
            elif k == 1:
                xacc[p, 0] = part[:h]
                send("xr", ("xr", p), out.at[hi], xtwo.at[p, 0, hi], at_x(1))
            else:
                xacc[p, 1] = part[h:]
                send("xr", ("xr", p), out.at[lo], xtwo.at[p, 1, lo], at_x(3))

    def add_x(p, way):
        arrive(("x1", p, way), xone.at[p, way])
        h = RTOK // 2
        mine = pl.ds(way * h, h)
        out = xsend.at[p, 2 * way, mine]
        out[...] = (xacc[p, way] + xone[p, way].astype(F32)).astype(BF16)
        send("xr", ("xr", p), out, xtwo.at[p, way, mine], at_x(1 + 2 * way))

    def zplace(p, part):
        return (
            pl.ds(2 * (part // 4), 2),
            slab(p),
            pl.ds(pl.multiple_of(x * XCOL + (part % 4) * ZCOL, ZCOL), ZCOL),
        )

    def sum_x(p):
        if XSUM[p]:
            arrive(("xr", p), xtwo.at[p, pl.ds(0, 2)])
            total = xown[p] + xtwo[p, 0].astype(F32) + xtwo[p, 1].astype(F32)
        else:
            arrive(("xr", p), xtwo.at[p])
            total = xown[p] + xtwo[p, 0].astype(F32) + xtwo[p, 1].astype(F32) + xtwo[p, 2].astype(F32)
        xown[p] = total
        for k in (4, 3, 5, 2, 6, 1, 7):
            part = (z + k) % NZ
            zsend[p, k - 1] = xown[
                p,
                pl.ds(pl.multiple_of((part // 4) * ZROW, ZROW), ZROW),
                pl.ds(pl.multiple_of((part % 4) * ZCOL, ZCOL), ZCOL),
            ].astype(BF16)
            send("zr", ("zr", p), zsend.at[p, k - 1], zrecv.at[p, k - 1], at_z(k))

    def sum_z(p):
        arrive(("zr", p), zrecv.at[p])
        total = xown[
            p,
            pl.ds(pl.multiple_of((z // 4) * ZROW, ZROW), ZROW),
            pl.ds(pl.multiple_of((z % 4) * ZCOL, ZCOL), ZCOL),
        ]
        for k in range(1, NZ):
            total = total + zrecv[p, k - 1].astype(F32)
        place = zplace(p, z)
        fin[place] = total.astype(BF16).reshape(2, SLAB, ZCOL)
        for k in (4, 3, 5, 2, 6, 1, 7):
            send("za", ("za", p), fin.at[place], fin.at[place], at_z(k))

    def xplace(p, k, start, size):
        return fin.at[
            pl.ds(start, size), slab(p), pl.ds(pl.multiple_of(((x + k) % NX) * XCOL, XCOL), XCOL)
        ]

    def gather_x(p):
        arrive(("za", p), zrecv.at[p])
        place = xplace(p, 0, 0, NY)
        for k in (1, 3) if XGATHER[p] else (2, 1, 3):
            send("xg", ("xg", p, k) if XGATHER[p] else ("xg", p), place, place, at_x(k))

    def pass_x(p, way):
        arrive(("xg", p, 1 + 2 * way), xplace(p, 3 - 2 * way, 0, NY))
        place = xplace(p, 3 - 2 * way, 2 * way, 2)
        send("xg", ("xh", p), place, place, at_x(1 + 2 * way))

    def finish(p):
        if XGATHER[p]:
            arrive(("xh", p), xplace(p, 2, 0, NY))
        else:
            arrive(("xg", p), xtwo.at[p])

    def weights(i):
        if i == 0:
            arrive("sx", xs)
            arrive("sg", gs)
            arrive("sd", agsib)
        if i == 3:
            arrive("hs", hsib)
        half = pl.ds(pl.multiple_of(dp * HALF, HALF), HALF)
        start, size = ((0, CUT), (CUT, CUT), (2 * CUT, BOTH - 2 * CUT), (0, HID))[i]
        mine, theirs, own, sib = (hall, hsib, gv, gs) if i == 3 else (ag, agsib, xv, xs)
        cols = slice(start, start + size)
        total = dot(mine[:, :, cols].reshape(TOK, size), own[:, :, half].reshape(TOK, HALF), ((0,), (0,)))
        total += dot(theirs[:, :, cols].reshape(TOK, size), sib[...].reshape(TOK, HALF), ((0,), (0,)))
        total = total.astype(BF16)
        if i == 2:
            gate_v[CUT:, :] = total[:rest]
            up_v[CUT:, :] = total[rest:]
        else:
            (gate_v, up_v, None, down_v)[i][:size, :] = total

    tasks = {
        "F": forward, "H": share, "E": elementwise, "K": hidden_send, "L": hidden_share, "C": contract,
        "X": add_x, "S": sum_x, "T": sum_z, "A": gather_x, "B": pass_x, "O": finish, "W": weights,
    }
    for name, *args in ORDER:
        tasks[name](*args)
    for out, ref in (
        ("yr", ysend), ("yg", ag.at[pl.ds(0, NY - 1)]), ("hg", hall.at[pl.ds(0, NY - 1)]), ("xr", xsend),
        ("zr", zsend), ("za", zrecv), ("xg", xsend), ("sx", xs), ("sg", gs), ("sd", agsib), ("hs", hsib),
    ):
        pltpu.make_async_copy(ref, ref, send_sem.at[sent[out]]).wait()


def write_out(*refs):
    sems = refs[8]
    copies = [pltpu.make_async_copy(refs[i], refs[4 + i], sems.at[i]) for i in range(4)]
    for copy in copies:
        copy.start()
    for copy in copies:
        copy.wait()


def body(layer_input, out_grad, w_gate, w_up, w_down):
    n_received = 5 + 4 * ROUNDS + sum(3 if ring else 1 for ring in XSUM + XGATHER)
    in_grad, gate_grad, up_grad, down_grad = pl.pallas_call(
        kernel,
        out_shape=(
            pltpu.VMEM((NY, OWN, WID), BF16),
            pltpu.VMEM((HID, HALF), BF16),
            pltpu.VMEM((HID, HALF), BF16),
            pltpu.VMEM((HID, HALF), BF16),
        ),
        in_specs=[pl.BlockSpec(memory_space=pltpu.HBM)] * 5,
        out_specs=[pl.BlockSpec(memory_space=pltpu.VMEM)] * 4,
        scratch_shapes=[
            pltpu.VMEM((NY, OWN, WID), BF16),
            pltpu.VMEM((NY, OWN, WID), BF16),
            pltpu.VMEM((BOTH, WID), BF16),
            pltpu.VMEM((HID, WID), BF16),
            pltpu.VMEM((NY, OWN, HALF), BF16),
            pltpu.VMEM((NY, OWN, HALF), BF16),
            pltpu.VMEM((ROUNDS, SLAB, PACK), F32),
            pltpu.VMEM((ROUNDS, NY - 1, SLAB, PACK), BF16),
            pltpu.VMEM((ROUNDS, NY - 1, SLAB, PACK), BF16),
            pltpu.VMEM((NY, OWN, BOTH), BF16),
            pltpu.VMEM((NY, OWN, BOTH), BF16),
            pltpu.VMEM((NY, OWN, PACK - BOTH), BF16),
            pltpu.VMEM((NY, OWN, PACK - BOTH), BF16),
            pltpu.VMEM((ROUNDS, RTOK, XCOL), F32),
            pltpu.VMEM((ROUNDS, 2, RTOK // 2, XCOL), F32),
            pltpu.VMEM((ROUNDS, NX - 1, RTOK, XCOL), BF16),
            pltpu.VMEM((ROUNDS, 2, RTOK // 2, XCOL), BF16),
            pltpu.VMEM((ROUNDS, NX - 1, RTOK, XCOL), BF16),
            pltpu.VMEM((ROUNDS, NZ - 1, ZROW, ZCOL), BF16),
            pltpu.VMEM((ROUNDS, NZ - 1, ZROW, ZCOL), BF16),
            pltpu.SemaphoreType.DMA((6,)),
            pltpu.SemaphoreType.DMA((11,)),
            pltpu.SemaphoreType.DMA((n_received,)),
        ],
        compiler_params=pltpu.CompilerParams(
            collective_id=0, has_side_effects=True, vmem_limit_bytes=58 * 2**20
        ),
    )(
        layer_input.reshape(NY, OWN, WID), out_grad.reshape(NY, OWN, WID), w_gate.T, w_up.T, w_down,
    )
    in_grad, gate_grad, up_grad, down_grad = pl.pallas_call(
        write_out,
        out_shape=[jax.ShapeDtypeStruct(a.shape, a.dtype) for a in (in_grad, gate_grad, up_grad, down_grad)],
        in_specs=[pl.BlockSpec(memory_space=pltpu.VMEM)] * 4,
        out_specs=[pl.BlockSpec(memory_space=pl.ANY)] * 4,
        scratch_shapes=[pltpu.SemaphoreType.DMA((4,))],
        compiler_params=pltpu.CompilerParams(vmem_limit_bytes=2**20),
    )(in_grad, gate_grad, up_grad, down_grad)
    return in_grad.reshape(TOK, WID), gate_grad.T, up_grad.T, down_grad


def solution(mesh):
    placed = (P("dp", "col"), P("dp", "col"), P("col", "row"), P("col", "row"), P("row", "col"))
    return jax.shard_map(
        body,
        mesh=mesh,
        in_specs=placed,
        out_specs=(
            P("dp", "col"),
            P(("col", "dp"), "row"),
            P(("col", "dp"), "row"),
            P("row", ("col", "dp")),
        ),
        check_vma=False,
    )
```

```python
import jax
import jax.numpy as jnp
from jax import lax
from jax.experimental import pallas as pl
from jax.experimental.pallas import tpu as pltpu
from jax.sharding import PartitionSpec as P

MESH = pl.DeviceIdType.MESH
BF16, F32 = jnp.bfloat16, jnp.float32
NX, NY, NZ = 4, 4, 8
TOK, WID, HID = 512, 2048, 448
CUT = 384
BOTH = 2 * HID
PACK = BOTH + 512
HALF = WID // 2
OWN = TOK // NY
ROUNDS = 8
BATCHES = ((0,), (1, 2), (3, 4), (5, 6), (7,))
SLAB = OWN // ROUNDS
RTOK = TOK // ROUNDS
XCOL = WID // NX
ZROW, ZCOL = RTOK // 2, XCOL // 4
EARLY = len(BATCHES[0]) * SLAB
PAIR = 2
XSUM = (1, 1, 0, 0, 0, 0, 0, 0)
XGATHER = (1, 1, 1, 0, 1, 1, 1, 0)
ORDER = (
    ("F", 0), ("F", 1), ("H",), ("E", 0), ("E", 1), ("F", 2), ("E", 2), ("C", 0), ("C", 1), ("E", 3), ("F", 3),
    ("X", 0, 0), ("X", 0, 1), ("E", 4), ("X", 1, 0), ("X", 1, 1), ("C", 2), ("C", 3), ("S", 0), ("S", 1),
    ("E", 5), ("F", 4), ("E", 6), ("S", 2), ("C", 4), ("C", 5), ("T", 0), ("S", 3), ("T", 1), ("E", 7),
    ("C", 6), ("T", 2), ("S", 4), ("C", 7), ("K",), ("S", 5), ("T", 3), ("S", 6), ("A", 0), ("A", 1), ("A", 2),
    ("T", 4), ("S", 7), ("T", 5), ("B", 0, 0), ("B", 0, 1), ("A", 3), ("B", 1, 0), ("B", 1, 1), ("T", 6),
    ("B", 2, 0), ("B", 2, 1), ("A", 4), ("T", 7), ("W", 0), ("A", 5), ("W", 1), ("L",), ("A", 6), ("W", 2),
    ("B", 4, 0), ("B", 4, 1), ("A", 7), ("W", 3), ("B", 5, 0), ("B", 5, 1), ("B", 6, 0), ("B", 6, 1), ("O", 0),
    ("O", 1), ("O", 2), ("O", 3), ("O", 4), ("O", 5), ("O", 6), ("O", 7),
)


def dot(left, right, dims):
    return lax.dot_general(left, right, (dims, ((), ())), preferred_element_type=F32)


def kernel(
    x_hbm, g_hbm, wg_hbm, wu_hbm, wd_hbm, fin, gate_v, up_v, down_v,
    xv, gv, wgu, wd, xs, gs, yown, ysend, yrecv, ag, agsib, hall, hsib,
    xown, xacc, xsend, xone, xtwo, zsend, zrecv, load_sem, send_sem, recv_sem,
):
    dp, row, y = lax.axis_index("dp"), lax.axis_index("row"), lax.axis_index("col")
    z, x = row // NX, row % NX

    def at_y(k):
        return (dp, row, (y + k) % NY)

    def at_x(k):
        return (dp, z * NX + (x + k) % NX, y)

    def at_z(k):
        return (dp, ((z + k) % NZ) * NX + x, y)

    sibling = (1 - dp, row, y)

    barrier = pltpu.get_barrier_semaphore()
    partners = (
        [at_y(k) for k in range(1, NY)] + [at_x(k) for k in range(1, NX)] + [at_z(k) for k in range(1, NZ)] + [sibling]
    )
    for partner in partners:
        pl.semaphore_signal(barrier, inc=1, device_id=partner, device_id_type=MESH)

    loads = {}

    def load(name, src, dst):
        n = loads.setdefault(name, len(loads))
        pltpu.make_async_copy(src, dst, load_sem.at[n]).start()

    def loaded(name, ref):
        if name in loads:
            pltpu.make_async_copy(ref, ref, load_sem.at[loads.pop(name)]).wait()

    early, late = pl.ds(0, EARLY), pl.ds(EARLY, OWN - EARLY)
    rest = HID - CUT
    load("x0", x_hbm.at[:, early], xv.at[:, early])
    load("w", wg_hbm.at[pl.ds(0, CUT)], wgu.at[pl.ds(0, CUT)])
    load("w", wu_hbm.at[pl.ds(0, CUT)], wgu.at[pl.ds(CUT, CUT)])
    load("w", wg_hbm.at[pl.ds(CUT, rest)], wgu.at[pl.ds(2 * CUT, rest)])
    load("w", wu_hbm.at[pl.ds(CUT, rest)], wgu.at[pl.ds(CUT + HID, rest)])
    load("g0", g_hbm.at[:, early], gv.at[:, early])
    load("wd", wd_hbm, wd)
    load("x1", x_hbm.at[:, late], xv.at[:, late])
    load("g1", g_hbm.at[:, late], gv.at[:, late])

    sent, received = {}, {}

    def send(out, name, src, dst, device):
        n, m = sent.setdefault(out, len(sent)), received.setdefault(name, len(received))
        pltpu.make_async_remote_copy(
            src_ref=src, dst_ref=dst, send_sem=send_sem.at[n], recv_sem=recv_sem.at[m],
            device_id=device, device_id_type=MESH,
        ).start()

    def arrive(name, ref):
        pltpu.make_async_copy(ref, ref, recv_sem.at[received[name]]).wait()

    def slab(p):
        return pl.ds(p * SLAB, SLAB)

    def forward(i):
        first, n = BATCHES[i][0], len(BATCHES[i]) * SLAB
        part = pl.ds(first * SLAB, n)
        loaded("x0", xv.at[:, early])
        loaded("w", wgu)
        if i > 0:
            loaded("x1", xv.at[:, late])
        a = jnp.concatenate([xv[(y + k) % NY, part] for k in range(NY)], axis=0)
        both = dot(a, wgu[...], ((1,), (1,)))
        loaded("g0", gv.at[:, early])
        loaded("wd", wd)
        if i > 0:
            loaded("g1", gv.at[:, late])
        a = jnp.concatenate([gv[(y + k) % NY, part] for k in range(NY)], axis=0)
        hid = dot(a, wd[...], ((1,), (1,)))
        hid = jnp.concatenate((hid, jnp.zeros((NY * n, PACK - BOTH - HID), F32)), axis=1)
        for p in BATCHES[i]:
            start = (p - first) * SLAB
            for k in range(1, NY):
                mine = slice(k * n + start, k * n + start + SLAB)
                ysend[p, k - 1, :, :BOTH] = both[mine].astype(BF16)
                ysend[p, k - 1, :, BOTH:] = hid[mine].astype(BF16)
            if p == 0:
                pl.semaphore_wait(barrier, len(partners))
            for k in (2, 1, 3):
                send("yr", ("yr", p), ysend.at[p, k - 1], yrecv.at[p, k - 1], at_y(k))
            yown[p, :, :BOTH] = both[start : start + SLAB]
            yown[p, :, BOTH:] = hid[start : start + SLAB]

    def share():
        other = pl.ds(pl.multiple_of((1 - dp) * HALF, HALF), HALF)
        send("sx", "sx", xv.at[:, :, other], xs, sibling)
        send("sg", "sg", gv.at[:, :, other], gs, sibling)

    def swiglu_back(gate, up, hid):
        sig = jax.nn.sigmoid(gate)
        act = gate * sig
        return (
            (act * up).astype(BF16),
            (hid * up * sig * (1.0 + gate * (1.0 - sig))).astype(BF16),
            (hid * act).astype(BF16),
        )

    def elementwise(p):
        arrive(("yr", p), yrecv.at[p])
        total = yown[p] + yrecv[p, 0].astype(F32) + yrecv[p, 1].astype(F32) + yrecv[p, 2].astype(F32)
        hidden, gate, up = swiglu_back(
            total[:, :CUT], total[:, CUT : 2 * CUT], total[:, BOTH : BOTH + CUT]
        )
        ag[y, slab(p), :CUT] = gate
        ag[y, slab(p), CUT : 2 * CUT] = up
        hall[y, slab(p), :CUT] = hidden
        rest = HID - CUT
        hidden, gate, up = swiglu_back(
            total[:, 2 * CUT : 2 * CUT + rest], total[:, 2 * CUT + rest : BOTH], total[:, BOTH + CUT : BOTH + HID]
        )
        ag[y, slab(p), 2 * CUT :] = jnp.concatenate((gate, up), axis=1)
        hall[y, slab(p), CUT:] = jnp.concatenate((hidden, jnp.zeros_like(hidden)), axis=1)
        own = ag.at[y, slab(p)]
        for k in (2, 1, 3):
            send("yg", ("yg", p), own, own, at_y(k))

    def hidden_send():
        for k in (2, 1, 3):
            send("hg", "hg", hall.at[y], hall.at[y], at_y(k))

    def hidden_share():
        arrive("hg", hall.at[pl.ds(0, NY - 1)])
        send("hs", "hs", hall, hsib, sibling)

    def contract(p):
        arrive(("yg", p), ag.at[pl.ds(0, NY - 1), slab(p)])
        if p % PAIR == PAIR - 1:
            part = pl.ds((p - PAIR + 1) * SLAB, PAIR * SLAB)
            send("sd", "sd", ag.at[:, part], agsib.at[:, part], sibling)
        a = jnp.concatenate([ag[k, slab(p)] for k in range(NY)], axis=0)
        h = RTOK // 2
        lo, hi = pl.ds(0, h), pl.ds(h, h)
        for k in (2, 1, 3, 0):
            block = pl.ds(pl.multiple_of(((x + k) % NX) * XCOL, XCOL), XCOL)
            part = dot(a, wgu[:, block], ((1,), (0,)))
            if k == 0:
                xown[p] = part
                continue
            out = xsend.at[p, k - 1]
            out[...] = part.astype(BF16)
            if not XSUM[p]:
                send("xr", ("xr", p), out, xtwo.at[p, k - 1], at_x(k))
            elif k == 2:
                send("xr", ("x1", p, 0), out.at[lo], xone.at[p, 0], at_x(1))
                send("xr", ("x1", p, 1), out.at[hi], xone.at[p, 1], at_x(3))
            elif k == 1:
                xacc[p, 0] = part[:h]
                send("xr", ("xr", p), out.at[hi], xtwo.at[p, 0, hi], at_x(1))
            else:
                xacc[p, 1] = part[h:]
                send("xr", ("xr", p), out.at[lo], xtwo.at[p, 1, lo], at_x(3))

    def add_x(p, way):
        arrive(("x1", p, way), xone.at[p, way])
        h = RTOK // 2
        mine = pl.ds(way * h, h)
        out = xsend.at[p, 2 * way, mine]
        out[...] = (xacc[p, way] + xone[p, way].astype(F32)).astype(BF16)
        send("xr", ("xr", p), out, xtwo.at[p, way, mine], at_x(1 + 2 * way))

    def zplace(p, part):
        return (
            pl.ds(2 * (part // 4), 2),
            slab(p),
            pl.ds(pl.multiple_of(x * XCOL + (part % 4) * ZCOL, ZCOL), ZCOL),
        )

    def sum_x(p):
        if XSUM[p]:
            arrive(("xr", p), xtwo.at[p, pl.ds(0, 2)])
            total = xown[p] + xtwo[p, 0].astype(F32) + xtwo[p, 1].astype(F32)
        else:
            arrive(("xr", p), xtwo.at[p])
            total = xown[p] + xtwo[p, 0].astype(F32) + xtwo[p, 1].astype(F32) + xtwo[p, 2].astype(F32)
        xown[p] = total
        for k in (4, 3, 5, 2, 6, 1, 7):
            part = (z + k) % NZ
            zsend[p, k - 1] = xown[
                p,
                pl.ds(pl.multiple_of((part // 4) * ZROW, ZROW), ZROW),
                pl.ds(pl.multiple_of((part % 4) * ZCOL, ZCOL), ZCOL),
            ].astype(BF16)
            send("zr", ("zr", p), zsend.at[p, k - 1], zrecv.at[p, k - 1], at_z(k))

    def sum_z(p):
        arrive(("zr", p), zrecv.at[p])
        total = xown[
            p,
            pl.ds(pl.multiple_of((z // 4) * ZROW, ZROW), ZROW),
            pl.ds(pl.multiple_of((z % 4) * ZCOL, ZCOL), ZCOL),
        ]
        for k in range(1, NZ):
            total = total + zrecv[p, k - 1].astype(F32)
        place = zplace(p, z)
        fin[place] = total.astype(BF16).reshape(2, SLAB, ZCOL)
        for k in (4, 3, 5, 2, 6, 1, 7):
            send("za", ("za", p), fin.at[place], fin.at[place], at_z(k))

    def xplace(p, k, start, size):
        return fin.at[
            pl.ds(start, size), slab(p), pl.ds(pl.multiple_of(((x + k) % NX) * XCOL, XCOL), XCOL)
        ]

    def gather_x(p):
        arrive(("za", p), zrecv.at[p])
        place = xplace(p, 0, 0, NY)
        for k in (1, 3) if XGATHER[p] else (2, 1, 3):
            send("xg", ("xg", p, k) if XGATHER[p] else ("xg", p), place, place, at_x(k))

    def pass_x(p, way):
        arrive(("xg", p, 1 + 2 * way), xplace(p, 3 - 2 * way, 0, NY))
        place = xplace(p, 3 - 2 * way, 2 * way, 2)
        send("xg", ("xh", p), place, place, at_x(1 + 2 * way))

    def finish(p):
        if XGATHER[p]:
            arrive(("xh", p), xplace(p, 2, 0, NY))
        else:
            arrive(("xg", p), xtwo.at[p])

    def weights(i):
        if i == 0:
            arrive("sx", xs)
            arrive("sg", gs)
            arrive("sd", agsib)
        if i == 3:
            arrive("hs", hsib)
        half = pl.ds(pl.multiple_of(dp * HALF, HALF), HALF)
        start, size = ((0, CUT), (CUT, CUT), (2 * CUT, BOTH - 2 * CUT), (0, HID))[i]
        mine, theirs, own, sib = (hall, hsib, gv, gs) if i == 3 else (ag, agsib, xv, xs)
        cols = slice(start, start + size)
        total = dot(mine[:, :, cols].reshape(TOK, size), own[:, :, half].reshape(TOK, HALF), ((0,), (0,)))
        total += dot(theirs[:, :, cols].reshape(TOK, size), sib[...].reshape(TOK, HALF), ((0,), (0,)))
        total = total.astype(BF16)
        if i == 2:
            gate_v[CUT:, :] = total[:rest]
            up_v[CUT:, :] = total[rest:]
        else:
            (gate_v, up_v, None, down_v)[i][:size, :] = total

    tasks = {
        "F": forward, "H": share, "E": elementwise, "K": hidden_send, "L": hidden_share, "C": contract,
        "X": add_x, "S": sum_x, "T": sum_z, "A": gather_x, "B": pass_x, "O": finish, "W": weights,
    }
    for name, *args in ORDER:
        tasks[name](*args)
    for out, ref in (
        ("yr", ysend), ("yg", ag.at[pl.ds(0, NY - 1)]), ("hg", hall.at[pl.ds(0, NY - 1)]), ("xr", xsend),
        ("zr", zsend), ("za", zrecv), ("xg", xsend), ("sx", xs), ("sg", gs), ("sd", agsib), ("hs", hsib),
    ):
        pltpu.make_async_copy(ref, ref, send_sem.at[sent[out]]).wait()


def write_out(*refs):
    sems = refs[8]
    copies = [pltpu.make_async_copy(refs[i], refs[4 + i], sems.at[i]) for i in range(4)]
    for copy in copies:
        copy.start()
    for copy in copies:
        copy.wait()


def body(layer_input, out_grad, w_gate, w_up, w_down):
    n_received = 5 + 4 * ROUNDS + sum(3 if ring else 1 for ring in XSUM + XGATHER)
    in_grad, gate_grad, up_grad, down_grad = pl.pallas_call(
        kernel,
        out_shape=(
            pltpu.VMEM((NY, OWN, WID), BF16),
            pltpu.VMEM((HID, HALF), BF16),
            pltpu.VMEM((HID, HALF), BF16),
            pltpu.VMEM((HID, HALF), BF16),
        ),
        in_specs=[pl.BlockSpec(memory_space=pltpu.HBM)] * 5,
        out_specs=[pl.BlockSpec(memory_space=pltpu.VMEM)] * 4,
        scratch_shapes=[
            pltpu.VMEM((NY, OWN, WID), BF16),
            pltpu.VMEM((NY, OWN, WID), BF16),
            pltpu.VMEM((BOTH, WID), BF16),
            pltpu.VMEM((HID, WID), BF16),
            pltpu.VMEM((NY, OWN, HALF), BF16),
            pltpu.VMEM((NY, OWN, HALF), BF16),
            pltpu.VMEM((ROUNDS, SLAB, PACK), F32),
            pltpu.VMEM((ROUNDS, NY - 1, SLAB, PACK), BF16),
            pltpu.VMEM((ROUNDS, NY - 1, SLAB, PACK), BF16),
            pltpu.VMEM((NY, OWN, BOTH), BF16),
            pltpu.VMEM((NY, OWN, BOTH), BF16),
            pltpu.VMEM((NY, OWN, PACK - BOTH), BF16),
            pltpu.VMEM((NY, OWN, PACK - BOTH), BF16),
            pltpu.VMEM((ROUNDS, RTOK, XCOL), F32),
            pltpu.VMEM((ROUNDS, 2, RTOK // 2, XCOL), F32),
            pltpu.VMEM((ROUNDS, NX - 1, RTOK, XCOL), BF16),
            pltpu.VMEM((ROUNDS, 2, RTOK // 2, XCOL), BF16),
            pltpu.VMEM((ROUNDS, NX - 1, RTOK, XCOL), BF16),
            pltpu.VMEM((ROUNDS, NZ - 1, ZROW, ZCOL), BF16),
            pltpu.VMEM((ROUNDS, NZ - 1, ZROW, ZCOL), BF16),
            pltpu.SemaphoreType.DMA((6,)),
            pltpu.SemaphoreType.DMA((11,)),
            pltpu.SemaphoreType.DMA((n_received,)),
        ],
        compiler_params=pltpu.CompilerParams(
            collective_id=0, has_side_effects=True, vmem_limit_bytes=58 * 2**20
        ),
    )(
        layer_input.reshape(NY, OWN, WID), out_grad.reshape(NY, OWN, WID), w_gate.T, w_up.T, w_down,
    )
    in_grad, gate_grad, up_grad, down_grad = pl.pallas_call(
        write_out,
        out_shape=[jax.ShapeDtypeStruct(a.shape, a.dtype) for a in (in_grad, gate_grad, up_grad, down_grad)],
        in_specs=[pl.BlockSpec(memory_space=pltpu.VMEM)] * 4,
        out_specs=[pl.BlockSpec(memory_space=pl.ANY)] * 4,
        scratch_shapes=[pltpu.SemaphoreType.DMA((4,))],
        compiler_params=pltpu.CompilerParams(vmem_limit_bytes=2**20),
    )(in_grad, gate_grad, up_grad, down_grad)
    return in_grad.reshape(TOK, WID), gate_grad.T, up_grad.T, down_grad


def solution(mesh):
    placed = (P("dp", "col"), P("dp", "col"), P("col", "row"), P("col", "row"), P("row", "col"))
    return jax.shard_map(
        body,
        mesh=mesh,
        in_specs=placed,
        out_specs=(
            P("dp", "col"),
            P(("col", "dp"), "row"),
            P(("col", "dp"), "row"),
            P("row", ("col", "dp")),
        ),
        check_vma=False,
    )
```
